256 devices in a mesh: ctx: 64 (over z_hi, y, x), head: 4 (over z_lo, core).
Axes of the slice: x: 4, y: 4, z: 8 (z_hi: 4, z_lo: 2; z = z_hi * 2 + z_lo), core: 2. Of those that a mesh axis runs over, the one named last changes fastest.
Arguments:
- queries: bfloat16 [16384, 4096], P('ctx', 'head'), may hold values from -30 to 30
- keys: bfloat16 [16384, 512], P('ctx', 'head'), may hold values from -30 to 30
- values: bfloat16 [16384, 512], P('ctx', 'head'), may hold values from -6 to 6
- lengths: int32 [32], replicated, may hold values from 1 to 2560, 16384 in all
- output_gradient: bfloat16 [16384, 4096], P('ctx', 'head'), may hold values from -6 to 6
Outputs:
- attn_out: bfloat16 [16384, 4096], P('ctx', 'head')
- query_grad: float32 [16384, 4096], P('ctx', 'head')
- key_grad: float32 [16384, 512], P('ctx', 'head')
- value_grad: float32 [16384, 512], P('ctx', 'head')
The draws below stay inside these ranges and needn't reach their ends.
Inputs may be any that keep to these rules, and one draw needn't show every extreme that they name: `lengths`: the documents fill the 16384 tokens in order; the longest has exactly 2560 tokens.
All inputs are finite; a program needn't handle non-finite values.
Results may differ from the reference program's by a relative error of at most 0.013.
Values may be sent and summed in bfloat16 or wider, within the bound.
A program may use at most 64 MiB of HBM per device.

```python
import math
import jax
import jax.numpy as jnp
import numpy as np
from jax import lax

QUERY_HEADS = 32
KEY_VALUE_HEADS = 4
HEAD_SIZE = 128
TOKENS_PER_SLICE = 256
PACKED_TOKENS = 16384
SPAN = 10
MAXDOC = 2560
DOCS = 32
N_CTX = 64


def draw_queries(key, part):
    key = jax.random.fold_in(key, 1)
    base_offset = jax.random.normal(key, (PACKED_TOKENS, QUERY_HEADS * HEAD_SIZE), jnp.float32)
    return jnp.clip(base_offset, -30.0, 30.0).astype(jnp.bfloat16)


def draw_keys(key, part):
    key = jax.random.fold_in(key, 2)
    base_offset = jax.random.normal(key, (PACKED_TOKENS, KEY_VALUE_HEADS * HEAD_SIZE), jnp.float32)
    return jnp.clip(base_offset, -30.0, 30.0).astype(jnp.bfloat16)


def block_scale(rng, extent, shards, smallest, largest):
    def one(axis_at, shards_of):
        heights = jax.random.uniform(jax.random.fold_in(jax.random.fold_in(rng, 6), axis_at), (shards_of,), jnp.float32, smallest / len(shards), largest / len(shards))
        return jnp.repeat(jnp.exp(heights), extent[axis_at] // shards_of).reshape((-1,) + (1,) * (len(extent) - axis_at - 1))

    factor_of = one(*shards[0])
    for cut in shards[1:]:
        factor_of = factor_of * one(*cut)
    return factor_of


def split_up(amount, total, limit, skew):
    weights = [(1 << 20) // math.isqrt(standing ** skew) + 1 for standing in range(2, amount + 1)]
    rest, holding = total - limit - (amount - 1), [1] * (amount - 1)
    while rest > 0:
        free = [i for i in range(amount - 1) if holding[i] < limit]
        pool, left = sum([weights[i] for i in free]), rest
        for i in free:
            addition = min(limit - holding[i], max(1, left * weights[i] // pool), rest)
            holding[i] = holding[i] + addition
            rest = rest - addition
    return np.array([limit] + holding)


def ragged_sizes(rng, amount, total, most, lean):
    if amount == 2:
        one = jax.random.randint(rng, (), max(1, total - most), min(most, total - 1) + 1)
        return jnp.stack([one, total - one])
    sizes = jnp.asarray(split_up(amount, total, most, lean), jnp.int32)
    couples = (amount - 1) // 2
    giver, receiver = sizes[1:1 + 2 * couples:2], sizes[2:2 + 2 * couples:2]
    slack = jnp.minimum(giver - 1, most - receiver)
    passed = jax.random.randint(jax.random.fold_in(rng, 1), (couples,), 0, 1 << 20) % (slack + 1)
    sizes = sizes.at[1:1 + 2 * couples:2].set(giver - passed).at[2:2 + 2 * couples:2].set(receiver + passed)
    return sizes[jax.random.permutation(jax.random.fold_in(rng, 2), amount)]


def scatter_about(own_key, shape, scale, reach, cuts=(), kind=jnp.bfloat16):
    drawn = jax.random.normal(own_key, shape, jnp.float32) * scale
    if len(cuts) > 0:
        drawn = block_scale(own_key, shape, cuts, -0.22, 0.18) * drawn
    return jnp.clip(drawn, min=-reach, max=reach).astype(kind)


def setup_inputs(seed: int = 0) -> dict:
    streams_of = jax.random.split(jax.random.key(seed), 6)
    queries = draw_queries(jax.random.fold_in(streams_of[5], 71), 0)
    keys = draw_keys(jax.random.fold_in(streams_of[5], 71), 0)
    values = scatter_about(streams_of[2], (PACKED_TOKENS, KEY_VALUE_HEADS * HEAD_SIZE), 1.0, 6.0, ((0, 64), (1, 4)))
    lengths = ragged_sizes(streams_of[3], DOCS, PACKED_TOKENS, MAXDOC, 2).astype(jnp.int32)
    output_gradient = scatter_about(streams_of[4], (PACKED_TOKENS, QUERY_HEADS * HEAD_SIZE), 1.0, 6.0, ((0, 64), (1, 4)))
    return dict(queries=queries, keys=keys, values=values, lengths=lengths, output_gradient=output_gradient)


neg_big = -1e30


def doc_of(lengths, positions):
    ends = jnp.cumsum(lengths).astype(jnp.int32)
    found = jnp.sum((positions[:, None] >= ends[None, :]).astype(jnp.int32), axis=1)
    return jnp.where(positions >= 0, found, -1).astype(jnp.int32)


def reference(queries, keys, values, lengths, output_gradient):
    group_members = QUERY_HEADS // KEY_VALUE_HEADS
    factor = HEAD_SIZE ** -0.5
    window_width = (SPAN + 1) * TOKENS_PER_SLICE
    padding_amount = SPAN * TOKENS_PER_SLICE
    key_padding = jnp.concatenate([jnp.zeros((padding_amount, KEY_VALUE_HEADS * HEAD_SIZE), jnp.float32), keys.astype(jnp.float32)], 0)
    value_padding = jnp.concatenate([jnp.zeros((padding_amount, KEY_VALUE_HEADS * HEAD_SIZE), jnp.float32), values.astype(jnp.float32)], 0)
    all_pos = jnp.arange(PACKED_TOKENS + padding_amount, dtype=jnp.int32) - padding_amount
    all_doc = doc_of(lengths, all_pos)

    def one_shard(acc, shard):
        start_position = (shard * TOKENS_PER_SLICE).astype(jnp.int32)
        current_query = lax.dynamic_slice_in_dim(queries, start_position, TOKENS_PER_SLICE, 0).astype(jnp.float32).reshape(TOKENS_PER_SLICE, KEY_VALUE_HEADS, group_members, HEAD_SIZE)
        current_gradient = lax.dynamic_slice_in_dim(output_gradient, start_position, TOKENS_PER_SLICE, 0).astype(jnp.float32).reshape(TOKENS_PER_SLICE, KEY_VALUE_HEADS, group_members, HEAD_SIZE)
        current_key = lax.dynamic_slice_in_dim(key_padding, start_position, window_width, 0).reshape(window_width, KEY_VALUE_HEADS, HEAD_SIZE)
        current_value = lax.dynamic_slice_in_dim(value_padding, start_position, window_width, 0).reshape(window_width, KEY_VALUE_HEADS, HEAD_SIZE)
        q_pos = lax.dynamic_slice_in_dim(all_pos, start_position + padding_amount, TOKENS_PER_SLICE, 0)
        q_doc = lax.dynamic_slice_in_dim(all_doc, start_position + padding_amount, TOKENS_PER_SLICE, 0)
        k_pos = lax.dynamic_slice_in_dim(all_pos, start_position, window_width, 0)
        k_doc = lax.dynamic_slice_in_dim(all_doc, start_position, window_width, 0)
        allowed = (q_doc[:, None] == k_doc[None, :]) & (k_pos[None, :] <= q_pos[:, None])
        scores = jnp.einsum("tkgd,skd->kgts", current_query, current_key) * factor
        scores = jnp.where(allowed, scores, neg_big)
        peak = jnp.max(scores, axis=-1)
        terms = jnp.where(allowed, jnp.exp(scores - peak[..., None]), 0.0)
        total = jnp.sum(terms, axis=-1)
        probs = terms / total[..., None]
        probabilities_reduced = lax.optimization_barrier(probs.astype(jnp.bfloat16)).astype(jnp.float32)
        full_out = jnp.einsum("kgts,skd->tkgd", probabilities_reduced, current_value)
        result = full_out.astype(jnp.bfloat16)
        slope = jnp.einsum("tkgd,skd->kgts", current_gradient, current_value)
        delta = jnp.einsum("tkgd,tkgd->kgt", current_gradient, full_out)
        score_gradient = lax.optimization_barrier((probs * (slope - delta[..., None]) * factor).astype(jnp.bfloat16)).astype(jnp.float32)
        q_grad = jnp.einsum("kgts,skd->tkgd", score_gradient, current_key)
        key_gradient = jnp.einsum("iofz,fion->zin", score_gradient, current_query).reshape(window_width, KEY_VALUE_HEADS * HEAD_SIZE)
        value_gradient = jnp.einsum("iofz,fion->zin", probabilities_reduced, current_gradient).reshape(window_width, KEY_VALUE_HEADS * HEAD_SIZE)
        older = lax.dynamic_slice_in_dim(acc, start_position, window_width, 1)
        acc = lax.dynamic_update_slice_in_dim(acc, older + jnp.stack([key_gradient, value_gradient]), start_position, 1)
        return acc, (result.reshape(TOKENS_PER_SLICE, QUERY_HEADS * HEAD_SIZE), q_grad.reshape(TOKENS_PER_SLICE, QUERY_HEADS * HEAD_SIZE))

    starting_accumulator = jnp.zeros((2, PACKED_TOKENS + padding_amount, KEY_VALUE_HEADS * HEAD_SIZE), jnp.float32)
    acc, (outputs, q_grads) = lax.scan(one_shard, starting_accumulator, jnp.arange(N_CTX, dtype=jnp.int32))
    attn_out = outputs.reshape(PACKED_TOKENS, QUERY_HEADS * HEAD_SIZE)
    query_grad = q_grads.reshape(PACKED_TOKENS, QUERY_HEADS * HEAD_SIZE)
    return attn_out, query_grad, acc[0, padding_amount:], acc[1, padding_amount:]
```

```python
import jax
import jax.numpy as jnp
from jax import lax
from jax.experimental import pallas as pl
from jax.experimental.pallas import tpu as pltpu
from jax.sharding import PartitionSpec as P

HEADS = 8
TOK = 256
DIM = 128
BLOCKS = 11
SLOTS = 15
FACTOR = DIM ** -0.5
EXP2 = FACTOR * 1.4426950408889634
NEG = -1e30
MESH = pl.DeviceIdType.MESH
F32, BF16 = jnp.float32, jnp.bfloat16

FETCH = ((0, 0), (1, 0), (0, 1), (0, 3), (2, 0), (1, 1), (1, 3), (0, 2), (2, 1), (2, 3), (1, 2), (3, 1), (3, 2), (2, 2))
RETURN = ((3, 1), (3, 2), (2, 2), (2, 1), (2, 3), (2, 0), (1, 2), (1, 1), (1, 3), (1, 0), (0, 2), (0, 1), (0, 3), (0, 0))


def dot_nt(a, b):
    return lax.dot_general(a, b, (((1,), (1,)), ((), ())), preferred_element_type=F32)


def dot_nn(a, b):
    return lax.dot_general(a, b, (((1,), (0,)), ((), ())), preferred_element_type=F32)


def pick(table, column, step):
    value = jnp.int32(0)
    for at, entry in enumerate(table):
        if entry[column]:
            value = value + entry[column] * (step == at).astype(jnp.int32)
    return value


def kernel(q, k, v, lengths, g, out, dq, dk, dv,
           kb, vb, s_sc, d_sc, m_sc, dl_sc, acc_q, qt, gt, th, bias,
           gk, gv, mid, side, row, tri,
           f_send, f_recv, c_send, c_recv, o_send, mid_recv, side_recv, row_recv, tri_send, tri_recv, far_send):
    me = lax.axis_index("ctx")
    size = lax.axis_size("ctx")
    x = me % 4
    y = (me // 4) % 4
    plane = me // 16
    base = me - x
    right, left = base + (x + 1) % 4, base + (x + 3) % 4

    def at_row(planes, r, c):
        return ((me // 16 + planes + size // 16) % (size // 16)) * 16 + r * 4 + c

    def slot(kk, j, col):
        return (4 * kk + j - 4 * ((col + j) // 4) + SLOTS) % SLOTS

    def remote(src, dst, send, recv, ctx):
        return pltpu.make_async_remote_copy(src_ref=src, dst_ref=dst, send_sem=send, recv_sem=recv,
                                            device_id={"ctx": ctx}, device_id_type=MESH)


    def far_pairs(act):
        for r in (1, 2, 3):
            for c in (0, 1):
                act((y == 0) & (x >= 2 + c), at_row(0, r, c), r, c)
        for c in (0, 1):
            act((y == 1) & (x >= 2 + c), at_row(1, 0, c), 0, c)

    barrier = pltpu.get_barrier_semaphore()

    def greet(ctx):
        pl.semaphore_signal(barrier, inc=1, device_id={"ctx": ctx}, device_id_type=MESH)

    for ctx in (right, left, (me + 4) % size, (me + size - 4) % size, (me + 8) % size, (me + size - 8) % size):
        greet(ctx)
    far_pairs(lambda on, ctx, r, c: pl.when(on)(lambda: greet(ctx)))
    for c in (0, 1):
        for s in (2 + c, 3) if c == 0 else (3,):
            @pl.when((x == c) & (y > 0))
            def _():
                greet(at_row(0, 0, s))

            @pl.when((x == c) & (y == 0))
            def _():
                greet(at_row(-1, 1, s))
    given = jnp.where(x >= 2, x - 1, 0) * jnp.where(y == 0, 3, jnp.where(y == 1, 1, 0))
    taken = jnp.where(x <= 1, 2 - x, 0)
    pl.semaphore_wait(barrier, 6 + given + taken)

    def column_copies(kk):
        ctx = (me + 4 * kk) % size
        return [remote(src, buf.at[4 * kk], c_send.at[n, kk], f_recv.at[n, 4 * kk], ctx)
                for n, (src, buf) in enumerate(((k, kb), (v, vb)))]

    def row_copies(kk):
        copies = []
        for n, buf in enumerate((kb, vb)):
            for side_no, (j, ctx) in enumerate(((1, right), (3, left))):
                to = slot(kk, j, x)
                copies.append(remote(buf.at[4 * kk], buf.at[to], f_send.at[n, kk, side_no], f_recv.at[n, to], ctx))
        return copies

    def onward_key(kk):
        col = (x + 3) % 4
        to = slot(kk, 2, col)
        return remote(kb.at[slot(kk, 1, col)], kb.at[to], f_send.at[0, kk, 2], f_recv.at[0, to], right)

    def onward_value(kk):
        col = (x + 1) % 4
        to = slot(kk, 2, col)
        return remote(vb.at[slot(kk, 3, col)], vb.at[to], f_send.at[1, kk, 2], f_recv.at[1, to], left)

    def far_copies(r, c, ctx):
        src = (4 * (3 - r)) if r else 0
        to = 12 + (c - x)
        return [remote(buf.at[src], buf.at[to], far_send.at[n, (r + 3) % 4 if r else 2, c], f_recv.at[n, to], ctx)
                for n, buf in enumerate((kb, vb))]

    def start_far(rows):
        def act(on, ctx, r, c):
            if r in rows:
                @pl.when(on)
                def _():
                    for copy in far_copies(r, c, ctx):
                        copy.start()
        far_pairs(act)

    for kk in (1, 2):
        for copy in column_copies(kk):
            copy.start()
    kb[0] = k[...]
    vb[0] = v[...]
    for copy in row_copies(0):
        copy.start()
    start_far((3, 0))

    start = jnp.full((TOK, DIM), -1, jnp.int32) * (me * TOK)
    token = lax.broadcasted_iota(jnp.int32, (TOK, DIM), 0)
    end = -me * TOK
    for doc in range(lengths.shape[0]):
        end = end + lengths[doc]
        start = jnp.where(token >= end, end, start)
    th[...] = start
    for h in range(HEADS):
        cols = slice(h * DIM, (h + 1) * DIM)
        qt[h] = q[:, cols].T
        gt[h] = g[:, cols].T
    m_sc[...] = jnp.full_like(m_sc, NEG)

    def arrived(at):
        for n, buf in enumerate((kb, vb)):
            remote(buf.at[at], buf.at[at], f_send.at[0, 0, 0], f_recv.at[n, at], right).wait_recv()

    def scores(d):
        key_at = lax.broadcasted_iota(jnp.int32, (TOK, DIM), 1) - d * TOK
        query_at = lax.broadcasted_iota(jnp.int32, (TOK, DIM), 0)
        for part in (0, 1):
            at = key_at + part * DIM
            seen = (at >= th[...]) & (at <= query_at)
            bias[:, part * DIM:(part + 1) * DIM] = jnp.where(seen, 0.0, NEG)
        key, value = kb[d], vb[d]
        for h in range(HEADS):
            cols = slice(h * DIM, (h + 1) * DIM)
            s = dot_nt(q[:, cols], key) + bias[...]
            s_sc[h, d] = s
            m_sc[h] = jnp.maximum(m_sc[h], jnp.maximum(s[:, :DIM], s[:, DIM:]))
            d_sc[h, d] = dot_nt(g[:, cols], value)

    def valid(kk, j):
        wraps = (j > x).astype(jnp.int32)
        d = 4 * kk + j - 4 * wraps
        return (d >= 0) & (d < BLOCKS), d

    def fetch_step(step, _):
        kk, j = pick(FETCH, 0, step), pick(FETCH, 1, step)
        ok, d = valid(kk, j)
        there = (d + SLOTS) % SLOTS

        @pl.when((step > 0) & (ok | (kk < 3)))
        def _():
            arrived(there)

        @pl.when((j == 0) & (kk > 0))
        def _():
            for copy in row_copies(kk):
                copy.start()

        @pl.when((j == 0) & (kk == 1))
        def _():
            start_far((2,))

        @pl.when((j == 0) & (kk == 2))
        def _():
            start_far((1,))

        @pl.when((j == 1) & (kk < 3))
        def _():
            onward_key(kk).start()

        @pl.when((j == 3) & (kk < 3))
        def _():
            onward_value(kk).start()

        @pl.when(ok)
        def _():
            scores(there)

        return 0

    lax.fori_loop(0, len(FETCH), fetch_step, 0)

    def finish_head(h, _):
        m = jnp.max(m_sc[h], axis=1, keepdims=True)
        total = jnp.zeros((TOK, 2 * DIM), F32)
        ones = jnp.ones((TOK, DIM), BF16)
        for d in range(BLOCKS):
            p = jnp.exp2((s_sc[h, d] - m) * EXP2).astype(BF16)
            total = total + dot_nn(p, jnp.concatenate([vb[d], ones], 1))
        norm = total[:, DIM:]
        full = total[:, :DIM] / norm
        acc_q[h] = full
        m_sc[h] = m * EXP2 + jnp.log2(norm)
        return 0

    lax.fori_loop(0, HEADS, finish_head, 0)
    for h in range(HEADS):
        cols = slice(h * DIM, (h + 1) * DIM)
        full = acc_q[h]
        out[:, cols] = full.astype(BF16)
        delta = jnp.sum(full * g[:, cols].astype(F32), axis=1, keepdims=True)
        dl_sc[h] = jnp.broadcast_to(delta, (TOK, DIM))
    acc_q[...] = jnp.zeros_like(acc_q)

    def gradients(d):
        key = kb[d]
        key_part = value_part = None
        for h in range(HEADS):
            lse, delta = m_sc[h], dl_sc[h]
            p = jnp.exp2(s_sc[h, d] * EXP2 - jnp.concatenate([lse, lse], 1))
            ds = (p * (d_sc[h, d] - jnp.concatenate([delta, delta], 1))).astype(BF16)
            acc_q[h] += dot_nn(ds, key)
            a, b = dot_nn(qt[h], ds), dot_nn(gt[h], p.astype(BF16))
            key_part = a if h == 0 else key_part + a
            value_part = b if h == 0 else value_part + b
        gk[d] = key_part.astype(BF16)
        gv[d] = value_part.astype(BF16)

    def add(ref, at, *others):
        total = ref[at].astype(F32)
        for other in others:
            total = total + other.astype(F32)
        ref[at] = total.astype(BF16)

    def mid_copy(n, kk, at):
        buf, ctx = ((gk, left), (gv, right))[n]
        return remote(buf.at[at], mid.at[n, kk], o_send.at[n, kk, 2], mid_recv.at[n, kk], ctx)

    def side_copies(kk, at, side_no, ctx):
        return [remote(buf.at[at], side.at[n, kk, side_no], o_send.at[n, kk, side_no], side_recv.at[n, kk, side_no], ctx)
                for n, buf in enumerate((gk, gv))]

    def home_copies(kk):
        ctx = (me + size - 4 * kk) % size
        return [remote(buf.at[4 * kk], row.at[n, kk], c_send.at[n, kk], row_recv.at[n, kk], ctx)
                for n, buf in enumerate((gk, gv))]

    def tri_copies(d):
        col = 12 + x - d
        where = jnp.where(y == 0, at_row(-1, 1, col), at_row(0, 0, col))
        index = jnp.where(y == 0, 2, y - 1)
        return [remote(buf.at[d], tri.at[n, index, x], tri_send.at[n, d - 9], tri_recv.at[n, index, x], where)
                for n, buf in enumerate((gk, gv))]

    def take_tri(kk):
        index = 2 - kk
        for c in (0, 1):
            @pl.when((x >= 2 + c) & ((y == 0) | ((y == 1) & (kk == 0))))
            def _():
                for n, buf in enumerate((gk, gv)):
                    remote(tri.at[n, index, c], tri.at[n, index, c], tri_send.at[n, 0], tri_recv.at[n, index, c],
                           right).wait_recv()
                    add(buf, 4 * kk, tri[n, index, c])

    def return_step(step, _):
        kk, j = pick(RETURN, 0, step), pick(RETURN, 1, step)
        ok, d = valid(kk, j)
        there = (d + SLOTS) % SLOTS

        @pl.when(ok)
        def _():
            gradients(there)

        @pl.when(jnp.logical_not(ok) & (kk < 3))
        def _():
            gk[there] = jnp.zeros((DIM, TOK), BF16)
            gv[there] = jnp.zeros((DIM, TOK), BF16)

        @pl.when((kk == 3) & ok)
        def _():
            for copy in tri_copies(there):
                copy.start()

        @pl.when((j == 2) & (kk < 3))
        def _():
            mid_copy(0, kk, there).start()
            mid_copy(1, kk, there).start()

        @pl.when((j == 1) & (kk < 3))
        def _():
            mid_copy(0, kk, there).wait_recv()
            add(gk, there, mid[0, kk])
            for copy in side_copies(kk, there, 0, left):
                copy.start()

        @pl.when((j == 3) & (kk < 3))
        def _():
            mid_copy(1, kk, there).wait_recv()
            add(gv, there, mid[1, kk])
            for copy in side_copies(kk, there, 1, right):
                copy.start()

        @pl.when(j == 0)
        def _():
            for side_no in (0, 1):
                for copy in side_copies(kk, there, side_no, right):
                    copy.wait_recv()
            for n, buf in enumerate((gk, gv)):
                add(buf, there, side[n, kk, 0], side[n, kk, 1])
            take_tri(kk)

            @pl.when(kk > 0)
            def _():
                for copy in home_copies(kk):
                    copy.start()

        return 0

    for kk in (1, 2):
        for copy in column_copies(kk):
            copy.wait_send()
    lax.fori_loop(0, len(RETURN), return_step, 0)

    for h in range(HEADS):
        dq[:, h * DIM:(h + 1) * DIM] = (acc_q[h] * FACTOR).astype(BF16)
    for kk in (1, 2):
        for copy in home_copies(kk):
            copy.wait_recv()
    for n, (buf, to) in enumerate(((gk, dk), (gv, dv))):
        total = buf[0].astype(F32) + row[n, 1].astype(F32) + row[n, 2].astype(F32)
        to[...] = (total * FACTOR if n == 0 else total).T

    def end_sends(kk, _):
        for copy in row_copies(kk):
            copy.wait_send()
        onward_key(kk).wait_send()
        onward_value(kk).wait_send()
        mid_copy(0, kk, 0).wait_send()
        mid_copy(1, kk, 0).wait_send()
        for side_no in (0, 1):
            for copy in side_copies(kk, 0, side_no, right):
                copy.wait_send()
        return 0

    lax.fori_loop(0, 3, end_sends, 0)
    for kk in (1, 2):
        for copy in home_copies(kk):
            copy.wait_send()

    def end_far(on, ctx, r, c):
        @pl.when(on)
        def _():
            for copy in far_copies(r, c, ctx):
                copy.wait_send()
    far_pairs(end_far)
    for d in (9, 10):
        @pl.when(x <= d - 9)
        def _():
            for copy in tri_copies(d):
                copy.wait_send()


def body(queries, keys, values, lengths, output_gradient):
    vmem = pl.BlockSpec(memory_space=pltpu.VMEM)
    wide = (TOK, HEADS * DIM)
    dma = pltpu.SemaphoreType.DMA
    out, dq, dk, dv = pl.pallas_call(
        kernel,
        out_shape=[
            jax.ShapeDtypeStruct(wide, BF16),
            jax.ShapeDtypeStruct(wide, BF16),
            jax.ShapeDtypeStruct((TOK, DIM), F32),
            jax.ShapeDtypeStruct((TOK, DIM), F32),
        ],
        in_specs=[vmem, vmem, vmem, pl.BlockSpec(memory_space=pltpu.SMEM), vmem],
        out_specs=[vmem] * 4,
        scratch_shapes=[
            pltpu.VMEM((SLOTS, TOK, DIM), BF16),
            pltpu.VMEM((SLOTS, TOK, DIM), BF16),
            pltpu.VMEM((HEADS, BLOCKS, TOK, TOK), F32),
            pltpu.VMEM((HEADS, BLOCKS, TOK, TOK), F32),
            pltpu.VMEM((HEADS, TOK, DIM), F32),
            pltpu.VMEM((HEADS, TOK, DIM), F32),
            pltpu.VMEM((HEADS, TOK, DIM), F32),
            pltpu.VMEM((HEADS, DIM, TOK), BF16),
            pltpu.VMEM((HEADS, DIM, TOK), BF16),
            pltpu.VMEM((TOK, DIM), jnp.int32),
            pltpu.VMEM((TOK, TOK), F32),
            pltpu.VMEM((SLOTS, DIM, TOK), BF16),
            pltpu.VMEM((SLOTS, DIM, TOK), BF16),
            pltpu.VMEM((2, 3, DIM, TOK), BF16),
            pltpu.VMEM((2, 3, 2, DIM, TOK), BF16),
            pltpu.VMEM((2, 3, DIM, TOK), BF16),
            pltpu.VMEM((2, 3, 2, DIM, TOK), BF16),
            dma((2, 3, 3)),
            dma((2, SLOTS)),
            dma((2, 3)),
            dma((2, 3)),
            dma((2, 3, 3)),
            dma((2, 3)),
            dma((2, 3, 2)),
            dma((2, 3)),
            dma((2, 2)),
            dma((2, 3, 2)),
            dma((2, 4, 2)),
        ],
        compiler_params=pltpu.CompilerParams(
            collective_id=0, has_side_effects=True, vmem_limit_bytes=62 << 20
        ),
    )(queries, keys, values, lengths, output_gradient)
    return out, dq.astype(F32), dk, dv


def solution(mesh):
    spec = P("ctx", "head")
    return jax.shard_map(
        body,
        mesh=mesh,
        in_specs=(spec, spec, spec, P(), spec),
        out_specs=(spec, spec, spec, spec),
        check_vma=False,
    )
```

```python
import jax
import jax.numpy as jnp
from jax import lax
from jax.experimental import pallas as pl
from jax.experimental.pallas import tpu as pltpu
from jax.sharding import PartitionSpec as P

HEADS = 8
TOK = 256
DIM = 128
BLOCKS = 11
SLOTS = 15
FACTOR = DIM ** -0.5
EXP2 = FACTOR * 1.4426950408889634
NEG = -1e30
MESH = pl.DeviceIdType.MESH
F32, BF16 = jnp.float32, jnp.bfloat16


def dot_nt(a, b):
    return lax.dot_general(a, b, (((1,), (1,)), ((), ())), preferred_element_type=F32)


def dot_nn(a, b):
    return lax.dot_general(a, b, (((1,), (0,)), ((), ())), preferred_element_type=F32)


def pick(table, column, step):
    value = jnp.int32(0)
    for at, entry in enumerate(table):
        if entry[column]:
            value = value + entry[column] * (step == at).astype(jnp.int32)
    return value


def kernel(q, k, v, lengths, g, out, dq, dk, dv,
           kb, vb, s_sc, d_sc, m_sc, dl_sc, acc_q, qt, gt, th, bias,
           gk, gv, mid, side, row, tri,
           f_send, f_recv, c_send, o_send, mid_recv, side_recv, row_recv, h_send, tri_recv):
    me = lax.axis_index("ctx")
    size = lax.axis_size("ctx")
    x = me % 4
    y = (me // 4) % 4
    base = me - x
    right, left = base + (x + 1) % 4, base + (x + 3) % 4
    stores = (kb, vb)

    def slot(kk, j, col):
        return (4 * kk + j - 4 * ((col + j) // 4) + SLOTS) % SLOTS

    def mine(kk, j):
        return slot(kk, j, (x + 4 - j) % 4)

    def remote(src, dst, send, recv, ctx):
        return pltpu.make_async_remote_copy(src_ref=src, dst_ref=dst, send_sem=send, recv_sem=recv,
                                            device_id={"ctx": ctx}, device_id_type=MESH)

    def start(*copies):
        for copy in copies:
            copy.start()

    def sent(*copies):
        for copy in copies:
            copy.wait_send()

    barrier = pltpu.get_barrier_semaphore()

    def greet(ctx):
        pl.semaphore_signal(barrier, inc=1, device_id={"ctx": ctx}, device_id_type=MESH)

    greet(right)
    greet(left)
    peers = 2
    for rows in (1, 2, 3):
        for sign in (1, -1):
            ctx = me + sign * 4 * rows
            on = (ctx >= 0) & (ctx < size)
            if rows == 3:
                on = on & (x <= 1)
            pl.when(on)(lambda ctx=ctx: greet(ctx))
            peers = peers + on.astype(jnp.int32)
    pl.semaphore_wait(barrier, peers)

    def column_copy(n, kk):
        src = (k, v)[n]
        return remote(src, stores[n].at[4 * kk], c_send.at[n, kk - 1], f_recv.at[n, 4 * kk], me + 4 * kk)

    def relay_copy(n):
        return remote(stores[n].at[4], stores[n].at[8], c_send.at[n, 2], f_recv.at[n, 8], me + 4)

    def far_copy(n, d):
        return remote(stores[n].at[d + 3], stores[n].at[d], c_send.at[n, d - 6], f_recv.at[n, d], me + 12)

    def row_copies(n, kk):
        buf = stores[n]
        copies = []
        for side_no, (j, ctx) in enumerate(((1, right), (3, left))):
            to = slot(kk, j, x)
            copies.append(remote(buf.at[4 * kk], buf.at[to], f_send.at[n, kk, side_no], f_recv.at[n, to], ctx))
        return copies

    def onward_copy(n, kk):
        buf, j, ctx = ((kb, 1, right), (vb, 3, left))[n]
        col = (x + 4 - j) % 4
        to = slot(kk, 2, col)
        return remote(buf.at[slot(kk, j, col)], buf.at[to], f_send.at[n, kk, 2], f_recv.at[n, to], ctx)

    def arrived(n, at):
        buf = stores[n]
        remote(buf.at[at], buf.at[at], f_send.at[n, 0, 0], f_recv.at[n, at], right).wait_recv()

    down = [(me + 4 < size), (me + 8 < size) & (y != 3), y == 0,
            (x == 0) & (me + 12 < size), (x <= 1) & (me + 12 < size)]

    @pl.when(down[0])
    def _():
        start(column_copy(0, 1), column_copy(1, 1))

    @pl.when(down[1])
    def _():
        start(column_copy(0, 2), column_copy(1, 2))

    kb[0] = k[...]
    vb[0] = v[...]
    start(*row_copies(0, 0), *row_copies(1, 0))

    for on, d in ((me < 4, 4), (me < 4, 8), ((me < 12) & (x == 0), 9), ((me < 12) & (x <= 1), 10)):
        @pl.when(on)
        def _():
            kb[d] = jnp.zeros((TOK, DIM), BF16)
            vb[d] = jnp.zeros((TOK, DIM), BF16)

    first = jnp.full((TOK, DIM), -1, jnp.int32) * (me * TOK)
    token = lax.broadcasted_iota(jnp.int32, (TOK, DIM), 0)
    end = -me * TOK
    for doc in range(lengths.shape[0]):
        end = end + lengths[doc]
        first = jnp.where(token >= end, end, first)
    th[...] = first
    for h in range(HEADS):
        cols = slice(h * DIM, (h + 1) * DIM)
        qt[h] = q[:, cols].T
        gt[h] = g[:, cols].T
    m_sc[...] = jnp.full_like(m_sc, NEG)

    def scores(d):
        key_at = lax.broadcasted_iota(jnp.int32, (TOK, DIM), 1) - d * TOK
        query_at = lax.broadcasted_iota(jnp.int32, (TOK, DIM), 0)
        for part in (0, 1):
            at = key_at + part * DIM
            seen = (at >= th[...]) & (at <= query_at)
            bias[:, part * DIM:(part + 1) * DIM] = jnp.where(seen, 0.0, NEG)
        key, value = kb[d], vb[d]
        for h in range(HEADS):
            cols = slice(h * DIM, (h + 1) * DIM)
            s = dot_nt(q[:, cols], key) + bias[...]
            s_sc[h, d] = s
            m_sc[h] = jnp.maximum(m_sc[h], jnp.maximum(s[:, :DIM], s[:, DIM:]))
            d_sc[h, d] = dot_nt(g[:, cols], value)

    def valid(kk, j):
        wraps = (j > x).astype(jnp.int32)
        d = 4 * kk + j - 4 * wraps
        return (d >= 0) & (d < BLOCKS), d

    def score_all(table):
        def step_of(step, _):
            ok, d = valid(pick(table, 0, step), pick(table, 1, step))

            @pl.when(ok)
            def _():
                scores(d)

            return 0

        lax.fori_loop(0, len(table), step_of, 0)

    score_all(((0, 0),))
    for n, j in ((0, 1), (1, 3)):
        arrived(n, mine(0, j))
        start(onward_copy(n, 0))
    for n in (0, 1):
        pl.when(me >= 4)(lambda: arrived(n, 4))
        start(*row_copies(n, 1))
        pl.when(down[2])(lambda: start(relay_copy(n)))
    arrived(1, mine(0, 1))
    arrived(0, mine(0, 3))
    pl.when(down[3])(lambda: start(far_copy(0, 9), far_copy(1, 9)))
    score_all(((1, 0), (0, 1)))
    for n in (0, 1):
        pl.when(me >= 4)(lambda: arrived(n, 8))
        start(*row_copies(n, 2))
    arrived(0, mine(0, 2))
    arrived(1, mine(0, 2))
    pl.when(down[4])(lambda: start(far_copy(0, 10), far_copy(1, 10)))
    score_all(((0, 3), (0, 2)))
    for n, j in ((0, 1), (1, 3)):
        arrived(n, mine(1, j))
        start(onward_copy(n, 1))
    arrived(1, mine(1, 1))
    arrived(0, mine(1, 3))
    score_all(((2, 0), (1, 1), (1, 3)))
    for n, j in ((0, 1), (1, 3)):
        arrived(n, mine(2, j))
        start(onward_copy(n, 2))
    arrived(1, mine(2, 1))
    arrived(0, mine(2, 3))
    arrived(0, mine(1, 2))
    arrived(1, mine(1, 2))
    score_all(((1, 2), (2, 1), (2, 3)))
    for d in (9, 10):
        @pl.when((me >= 12) & (x <= d - 9))
        def _():
            arrived(0, d)
            arrived(1, d)
    arrived(0, mine(2, 2))
    arrived(1, mine(2, 2))
    score_all(((3, 1), (3, 2), (2, 2)))

    def finish_head(h, _):
        m = jnp.max(m_sc[h], axis=1, keepdims=True)
        total = jnp.zeros((TOK, 2 * DIM), F32)
        ones = jnp.ones((TOK, DIM), BF16)
        for d in range(BLOCKS):
            p = jnp.exp2((s_sc[h, d] - m) * EXP2).astype(BF16)
            total = total + dot_nn(p, jnp.concatenate([vb[d], ones], 1))
        norm = total[:, DIM:]
        full = total[:, :DIM] / norm
        acc_q[h] = full
        m_sc[h] = m * EXP2 + jnp.log2(norm)
        return 0

    lax.fori_loop(0, HEADS, finish_head, 0)
    for h in range(HEADS):
        cols = slice(h * DIM, (h + 1) * DIM)
        full = acc_q[h]
        out[:, cols] = full.astype(BF16)
        delta = jnp.sum(full * g[:, cols].astype(F32), axis=1, keepdims=True)
        dl_sc[h] = jnp.broadcast_to(delta, (TOK, DIM))
    acc_q[...] = jnp.zeros_like(acc_q)

    def gradients(d):
        key = kb[d]
        key_part = value_part = None
        for h in range(HEADS):
            lse, delta = m_sc[h], dl_sc[h]
            p = jnp.exp2(s_sc[h, d] * EXP2 - jnp.concatenate([lse, lse], 1))
            ds = (p * (d_sc[h, d] - jnp.concatenate([delta, delta], 1))).astype(BF16)
            acc_q[h] += dot_nn(ds, key)
            a, b = dot_nn(qt[h], ds), dot_nn(gt[h], p.astype(BF16))
            key_part = a if h == 0 else key_part + a
            value_part = b if h == 0 else value_part + b
        gk[d] = key_part.astype(BF16)
        gv[d] = value_part.astype(BF16)

    grads = (gk, gv)

    def add(ref, at, *others):
        total = ref[at].astype(F32)
        for other in others:
            total = total + other.astype(F32)
        ref[at] = total.astype(BF16)

    def mid_copy(n, kk):
        return remote(grads[n].at[mine(kk, 2)], mid.at[n, kk], o_send.at[n, kk, 2], mid_recv.at[n, kk], (left, right)[n])

    def side_copy(n, kk, side_no):
        at, ctx = mine(kk, (1, 3)[side_no]), (left, right)[side_no]
        return remote(grads[n].at[at], side.at[n, kk, side_no], o_send.at[n, kk, side_no],
                      side_recv.at[n, kk, side_no], ctx)

    def home_copy(n, kk):
        return remote(grads[n].at[4 * kk], row.at[n, kk - 1], h_send.at[n, kk - 1], row_recv.at[n, kk - 1], me - 4 * kk)

    def tri_copy(n, d):
        return remote(grads[n].at[d], tri.at[n, d - 9], h_send.at[n, d - 7], tri_recv.at[n, d - 9], me - 12)

    def gradients_all(table):
        def step_of(step, _):
            kk, j = pick(table, 0, step), pick(table, 1, step)
            ok, d = valid(kk, j)
            there = (d + SLOTS) % SLOTS

            @pl.when(ok)
            def _():
                gradients(d)

            @pl.when(jnp.logical_not(ok) & (kk < 3))
            def _():
                gk[there] = jnp.zeros((DIM, TOK), BF16)
                gv[there] = jnp.zeros((DIM, TOK), BF16)

            return 0

        lax.fori_loop(0, len(table), step_of, 0)

    def pass_sides(kk):
        for n, j in ((0, 1), (1, 3)):
            mid_copy(n, kk).wait_recv()
            add(grads[n], mine(kk, j), mid[n, kk])
        start(side_copy(0, kk, 0), side_copy(1, kk, 0), side_copy(0, kk, 1), side_copy(1, kk, 1))

    def take_sides(kk):
        for n in (0, 1):
            side_copy(n, kk, 0).wait_recv()
            side_copy(n, kk, 1).wait_recv()
            add(grads[n], 4 * kk, side[n, kk, 0], side[n, kk, 1])
        if kk:
            pl.when(me >= 4 * kk)(lambda: start(home_copy(0, kk), home_copy(1, kk)))

    gradients_all(((3, 2), (3, 1)))
    for d in (10, 9):
        pl.when((me >= 12) & (x <= d - 9))(lambda: start(tri_copy(0, d), tri_copy(1, d)))
    gradients_all(((2, 2),))
    start(mid_copy(0, 2), mid_copy(1, 2))
    gradients_all(((2, 1), (2, 3), (1, 2)))
    start(mid_copy(0, 1), mid_copy(1, 1))
    gradients_all(((2, 0),))
    pass_sides(2)
    gradients_all(((1, 1), (1, 3)))
    pass_sides(1)
    gradients_all(((1, 0), (0, 2)))
    for d in (10, 9):
        if d == 9:
            take_sides(2)
            gradients_all(((0, 1), (0, 3)))

        @pl.when((me + 12 < size) & (x <= d - 9))
        def _():
            for n in (0, 1):
                tri_copy(n, d).wait_recv()
                grads[n][d + 3] = tri[n, d - 9]

        if d == 10:
            start(mid_copy(0, 0), mid_copy(1, 0))
    pass_sides(0)
    gradients_all(((0, 0),))
    take_sides(1)

    for h in range(HEADS):
        dq[:, h * DIM:(h + 1) * DIM] = (acc_q[h] * FACTOR).astype(BF16)
    take_sides(0)
    for kk in (1, 2):
        @pl.when(me + 4 * kk < size)
        def _():
            for n in (0, 1):
                home_copy(n, kk).wait_recv()
                add(grads[n], 0, row[n, kk - 1])
    dk[...] = (gk[0].astype(F32) * FACTOR).T
    dv[...] = gv[0].astype(F32).T

    for n in (0, 1):
        for at, copy in enumerate((column_copy(n, 1), column_copy(n, 2), relay_copy(n), far_copy(n, 9), far_copy(n, 10))):
            pl.when(down[at])(lambda: sent(copy))
        for kk in (0, 1, 2):
            sent(*row_copies(n, kk), onward_copy(n, kk), mid_copy(n, kk), side_copy(n, kk, 0), side_copy(n, kk, 1))
        for kk in (1, 2):
            pl.when(me >= 4 * kk)(lambda: sent(home_copy(n, kk)))
        for d in (9, 10):
            pl.when((me >= 12) & (x <= d - 9))(lambda: sent(tri_copy(n, d)))


def body(queries, keys, values, lengths, output_gradient):
    vmem = pl.BlockSpec(memory_space=pltpu.VMEM)
    wide = (TOK, HEADS * DIM)
    dma = pltpu.SemaphoreType.DMA
    out, dq, dk, dv = pl.pallas_call(
        kernel,
        out_shape=[
            jax.ShapeDtypeStruct(wide, BF16),
            jax.ShapeDtypeStruct(wide, BF16),
            jax.ShapeDtypeStruct((TOK, DIM), F32),
            jax.ShapeDtypeStruct((TOK, DIM), F32),
        ],
        in_specs=[vmem, vmem, vmem, pl.BlockSpec(memory_space=pltpu.SMEM), vmem],
        out_specs=[vmem] * 4,
        scratch_shapes=[
            pltpu.VMEM((SLOTS, TOK, DIM), BF16),
            pltpu.VMEM((SLOTS, TOK, DIM), BF16),
            pltpu.VMEM((HEADS, BLOCKS, TOK, TOK), F32),
            pltpu.VMEM((HEADS, BLOCKS, TOK, TOK), F32),
            pltpu.VMEM((HEADS, TOK, DIM), F32),
            pltpu.VMEM((HEADS, TOK, DIM), F32),
            pltpu.VMEM((HEADS, TOK, DIM), F32),
            pltpu.VMEM((HEADS, DIM, TOK), BF16),
            pltpu.VMEM((HEADS, DIM, TOK), BF16),
            pltpu.VMEM((TOK, DIM), jnp.int32),
            pltpu.VMEM((TOK, TOK), F32),
            pltpu.VMEM((SLOTS, DIM, TOK), BF16),
            pltpu.VMEM((SLOTS, DIM, TOK), BF16),
            pltpu.VMEM((2, 3, DIM, TOK), BF16),
            pltpu.VMEM((2, 3, 2, DIM, TOK), BF16),
            pltpu.VMEM((2, 2, DIM, TOK), BF16),
            pltpu.VMEM((2, 2, DIM, TOK), BF16),
            dma((2, 3, 3)),
            dma((2, SLOTS)),
            dma((2, 5)),
            dma((2, 3, 3)),
            dma((2, 3)),
            dma((2, 3, 2)),
            dma((2, 2)),
            dma((2, 4)),
            dma((2, 2)),
        ],
        compiler_params=pltpu.CompilerParams(
            collective_id=0, has_side_effects=True, vmem_limit_bytes=62 << 20
        ),
    )(queries, keys, values, lengths, output_gradient)
    return out, dq.astype(F32), dk, dv


def solution(mesh):
    spec = P("ctx", "head")
    return jax.shard_map(
        body,
        mesh=mesh,
        in_specs=(spec, spec, spec, P(), spec),
        out_specs=(spec, spec, spec, spec),
        check_vma=False,
    )
```

```python
import jax
import jax.numpy as jnp
from jax import lax
from jax.experimental import pallas as pl
from jax.experimental.pallas import tpu as pltpu
from jax.sharding import PartitionSpec as P

HEADS = 8
TOK = 256
DIM = 128
BLOCKS = 11
SLOTS = 15
FACTOR = DIM ** -0.5
EXP2 = FACTOR * 1.4426950408889634
NEG = -1e30
MESH = pl.DeviceIdType.MESH
F32, BF16 = jnp.float32, jnp.bfloat16


def dot_nt(a, b):
    return lax.dot_general(a, b, (((1,), (1,)), ((), ())), preferred_element_type=F32)


def dot_nn(a, b):
    return lax.dot_general(a, b, (((1,), (0,)), ((), ())), preferred_element_type=F32)


def pick(table, column, step):
    value = jnp.int32(0)
    for at, entry in enumerate(table):
        if entry[column]:
            value = value + entry[column] * (step == at).astype(jnp.int32)
    return value


def kernel(q, k, v, lengths, g, out, dq, dk, dv,
           kb, vb, s_sc, d_sc, m_sc, dl_sc, acc_q, qt, gt, th, bias,
           gk, gv, mid, side, row, tri,
           f_send, f_recv, c_send, o_send, mid_recv, side_recv, row_recv, h_send, tri_recv):
    me = lax.axis_index("ctx")
    size = lax.axis_size("ctx")
    x = me % 4
    y = (me // 4) % 4
    base = me - x
    right, left = base + (x + 1) % 4, base + (x + 3) % 4
    stores = (kb, vb)

    def slot(kk, j, col):
        return (4 * kk + j - 4 * ((col + j) // 4) + SLOTS) % SLOTS

    def mine(kk, j):
        return slot(kk, j, (x + 4 - j) % 4)

    def remote(src, dst, send, recv, ctx):
        return pltpu.make_async_remote_copy(src_ref=src, dst_ref=dst, send_sem=send, recv_sem=recv,
                                            device_id={"ctx": ctx}, device_id_type=MESH)

    def start(*copies):
        for copy in copies:
            copy.start()

    def sent(*copies):
        for copy in copies:
            copy.wait_send()

    barrier = pltpu.get_barrier_semaphore()

    def greet(ctx):
        pl.semaphore_signal(barrier, inc=1, device_id={"ctx": ctx}, device_id_type=MESH)

    greet(right)
    greet(left)
    peers = 2
    for rows in (1, 2, 3):
        for sign in (1, -1):
            ctx = me + sign * 4 * rows
            on = (ctx >= 0) & (ctx < size)
            if rows == 3:
                on = on & (x <= 1)
            pl.when(on)(lambda ctx=ctx: greet(ctx))
            peers = peers + on.astype(jnp.int32)
    pl.semaphore_wait(barrier, peers)

    def column_copy(n, kk):
        src = (k, v)[n]
        return remote(src, stores[n].at[4 * kk], c_send.at[n, kk - 1], f_recv.at[n, 4 * kk], me + 4 * kk)

    def relay_copy(n):
        return remote(stores[n].at[4], stores[n].at[8], c_send.at[n, 2], f_recv.at[n, 8], me + 4)

    def far_copy(n, d):
        return remote(stores[n].at[d + 3], stores[n].at[d], c_send.at[n, d - 6], f_recv.at[n, d], me + 12)

    def row_copies(n, kk):
        buf = stores[n]
        copies = []
        for side_no, (j, ctx) in enumerate(((1, right), (3, left))):
            to = slot(kk, j, x)
            copies.append(remote(buf.at[4 * kk], buf.at[to], f_send.at[n, kk, side_no], f_recv.at[n, to], ctx))
        return copies

    def onward_copy(n, kk):
        buf, j, ctx = ((kb, 1, right), (vb, 3, left))[n]
        col = (x + 4 - j) % 4
        to = slot(kk, 2, col)
        return remote(buf.at[slot(kk, j, col)], buf.at[to], f_send.at[n, kk, 2], f_recv.at[n, to], ctx)

    def arrived(n, at):
        buf = stores[n]
        remote(buf.at[at], buf.at[at], f_send.at[n, 0, 0], f_recv.at[n, at], right).wait_recv()

    down = [(me + 4 < size), (me + 8 < size) & (y != 3), y == 0,
            (x == 0) & (me + 12 < size), (x <= 1) & (me + 12 < size)]

    @pl.when(down[0])
    def _():
        start(column_copy(0, 1), column_copy(1, 1))

    @pl.when(down[1])
    def _():
        start(column_copy(0, 2), column_copy(1, 2))

    kb[0] = k[...]
    vb[0] = v[...]
    start(*row_copies(0, 0), *row_copies(1, 0))

    for on, d in ((me < 4, 4), (me < 4, 8), ((me < 12) & (x == 0), 9), ((me < 12) & (x <= 1), 10)):
        @pl.when(on)
        def _():
            kb[d] = jnp.zeros((TOK, DIM), BF16)
            vb[d] = jnp.zeros((TOK, DIM), BF16)

    first = jnp.full((TOK, DIM), -1, jnp.int32) * (me * TOK)
    token = lax.broadcasted_iota(jnp.int32, (TOK, DIM), 0)
    end = -me * TOK
    for doc in range(lengths.shape[0]):
        end = end + lengths[doc]
        first = jnp.where(token >= end, end, first)
    th[...] = first
    for h in range(HEADS):
        cols = slice(h * DIM, (h + 1) * DIM)
        qt[h] = q[:, cols].T
        gt[h] = g[:, cols].T
    m_sc[...] = jnp.full_like(m_sc, NEG)

    def scores(d):
        key_at = lax.broadcasted_iota(jnp.int32, (TOK, DIM), 1) - d * TOK
        query_at = lax.broadcasted_iota(jnp.int32, (TOK, DIM), 0)
        for part in (0, 1):
            at = key_at + part * DIM
            seen = (at >= th[...]) & (at <= query_at)
            bias[:, part * DIM:(part + 1) * DIM] = jnp.where(seen, 0.0, NEG)
        key, value = kb[d], vb[d]
        for h in range(HEADS):
            cols = slice(h * DIM, (h + 1) * DIM)
            s = dot_nt(q[:, cols], key) + bias[...]
            s_sc[h, d] = s
            m_sc[h] = jnp.maximum(m_sc[h], jnp.maximum(s[:, :DIM], s[:, DIM:]))
            d_sc[h, d] = dot_nt(g[:, cols], value)

    def valid(kk, j):
        wraps = (j > x).astype(jnp.int32)
        d = 4 * kk + j - 4 * wraps
        return (d >= 0) & (d < BLOCKS), d

    def score_all(table):
        def step_of(step, _):
            ok, d = valid(pick(table, 0, step), pick(table, 1, step))

            @pl.when(ok)
            def _():
                scores(d)

            return 0

        lax.fori_loop(0, len(table), step_of, 0)

    score_all(((0, 0),))
    for n, j in ((0, 1), (1, 3)):
        arrived(n, mine(0, j))
        start(onward_copy(n, 0))
    for n in (0, 1):
        pl.when(me >= 4)(lambda: arrived(n, 4))
        start(*row_copies(n, 1))
        pl.when(down[2])(lambda: start(relay_copy(n)))
    arrived(1, mine(0, 1))
    arrived(0, mine(0, 3))
    pl.when(down[3])(lambda: start(far_copy(0, 9), far_copy(1, 9)))
    score_all(((1, 0), (0, 1)))
    for n in (0, 1):
        pl.when(me >= 4)(lambda: arrived(n, 8))
        start(*row_copies(n, 2))
    arrived(0, mine(0, 2))
    arrived(1, mine(0, 2))
    pl.when(down[4])(lambda: start(far_copy(0, 10), far_copy(1, 10)))
    score_all(((0, 3), (0, 2)))
    for n, j in ((0, 1), (1, 3)):
        arrived(n, mine(1, j))
        start(onward_copy(n, 1))
    arrived(1, mine(1, 1))
    arrived(0, mine(1, 3))
    score_all(((2, 0), (1, 1), (1, 3)))
    for n, j in ((0, 1), (1, 3)):
        arrived(n, mine(2, j))
        start(onward_copy(n, 2))
    arrived(1, mine(2, 1))
    arrived(0, mine(2, 3))
    arrived(0, mine(1, 2))
    arrived(1, mine(1, 2))
    score_all(((1, 2), (2, 1), (2, 3)))
    for d in (9, 10):
        @pl.when((me >= 12) & (x <= d - 9))
        def _():
            arrived(0, d)
            arrived(1, d)
    arrived(0, mine(2, 2))
    arrived(1, mine(2, 2))
    score_all(((3, 1), (3, 2), (2, 2)))

    def finish_head(h, _):
        m = jnp.max(m_sc[h], axis=1, keepdims=True)
        total = jnp.zeros((TOK, 2 * DIM), F32)
        ones = jnp.ones((TOK, DIM), BF16)
        for d in range(BLOCKS):
            p = jnp.exp2((s_sc[h, d] - m) * EXP2).astype(BF16)
            total = total + dot_nn(p, jnp.concatenate([vb[d], ones], 1))
        norm = total[:, DIM:]
        full = total[:, :DIM] / norm
        acc_q[h] = full
        m_sc[h] = m * EXP2 + jnp.log2(norm)
        return 0

    lax.fori_loop(0, HEADS, finish_head, 0)
    for h in range(HEADS):
        cols = slice(h * DIM, (h + 1) * DIM)
        full = acc_q[h]
        out[:, cols] = full.astype(BF16)
        delta = jnp.sum(full * g[:, cols].astype(F32), axis=1, keepdims=True)
        dl_sc[h] = jnp.broadcast_to(delta, (TOK, DIM))
    acc_q[...] = jnp.zeros_like(acc_q)

    def gradients(d):
        key = kb[d]
        key_part = value_part = None
        for h in range(HEADS):
            lse, delta = m_sc[h], dl_sc[h]
            p = jnp.exp2(s_sc[h, d] * EXP2 - jnp.concatenate([lse, lse], 1))
            ds = (p * (d_sc[h, d] - jnp.concatenate([delta, delta], 1))).astype(BF16)
            acc_q[h] += dot_nn(ds, key)
            a, b = dot_nn(qt[h], ds), dot_nn(gt[h], p.astype(BF16))
            key_part = a if h == 0 else key_part + a
            value_part = b if h == 0 else value_part + b
        gk[d] = key_part.astype(BF16)
        gv[d] = value_part.astype(BF16)

    grads = (gk, gv)

    def add(ref, at, *others):
        total = ref[at].astype(F32)
        for other in others:
            total = total + other.astype(F32)
        ref[at] = total.astype(BF16)

    def mid_copy(n, kk):
        return remote(grads[n].at[mine(kk, 2)], mid.at[n, kk], o_send.at[n, kk, 2], mid_recv.at[n, kk], (left, right)[n])

    def side_copy(n, kk, side_no):
        at, ctx = mine(kk, (1, 3)[side_no]), (left, right)[side_no]
        return remote(grads[n].at[at], side.at[n, kk, side_no], o_send.at[n, kk, side_no],
                      side_recv.at[n, kk, side_no], ctx)

    def home_copy(n, kk):
        return remote(grads[n].at[4 * kk], row.at[n, kk - 1], h_send.at[n, kk - 1], row_recv.at[n, kk - 1], me - 4 * kk)

    def tri_copy(n, d):
        return remote(grads[n].at[d], tri.at[n, d - 9], h_send.at[n, d - 7], tri_recv.at[n, d - 9], me - 12)

    def gradients_all(table):
        def step_of(step, _):
            kk, j = pick(table, 0, step), pick(table, 1, step)
            ok, d = valid(kk, j)
            there = (d + SLOTS) % SLOTS

            @pl.when(ok)
            def _():
                gradients(d)

            @pl.when(jnp.logical_not(ok) & (kk < 3))
            def _():
                gk[there] = jnp.zeros((DIM, TOK), BF16)
                gv[there] = jnp.zeros((DIM, TOK), BF16)

            return 0

        lax.fori_loop(0, len(table), step_of, 0)

    def pass_sides(kk):
        for n, j in ((0, 1), (1, 3)):
            mid_copy(n, kk).wait_recv()
            add(grads[n], mine(kk, j), mid[n, kk])
        start(side_copy(0, kk, 0), side_copy(1, kk, 0), side_copy(0, kk, 1), side_copy(1, kk, 1))

    def take_sides(kk):
        for n in (0, 1):
            side_copy(n, kk, 0).wait_recv()
            side_copy(n, kk, 1).wait_recv()
            add(grads[n], 4 * kk, side[n, kk, 0], side[n, kk, 1])
        if kk:
            pl.when(me >= 4 * kk)(lambda: start(home_copy(0, kk), home_copy(1, kk)))

    gradients_all(((3, 2), (3, 1)))
    for d in (10, 9):
        pl.when((me >= 12) & (x <= d - 9))(lambda: start(tri_copy(0, d), tri_copy(1, d)))
    gradients_all(((2, 2),))
    start(mid_copy(0, 2), mid_copy(1, 2))
    gradients_all(((1, 2),))
    start(mid_copy(0, 1), mid_copy(1, 1))
    gradients_all(((2, 1), (2, 3)))
    pass_sides(2)
    gradients_all(((1, 1), (1, 3)))
    pass_sides(1)
    gradients_all(((0, 2), (2, 0), (1, 0), (0, 1), (0, 3), (0, 0)))
    take_sides(2)

    @pl.when((me + 12 < size) & (x <= 1))
    def _():
        for n in (0, 1):
            tri_copy(n, 10).wait_recv()
            grads[n][13] = tri[n, 1]

    start(mid_copy(0, 0), mid_copy(1, 0))
    take_sides(1)

    @pl.when((me + 12 < size) & (x <= 0))
    def _():
        for n in (0, 1):
            tri_copy(n, 9).wait_recv()
            grads[n][12] = tri[n, 0]

    pass_sides(0)

    for h in range(HEADS):
        dq[:, h * DIM:(h + 1) * DIM] = (acc_q[h] * FACTOR).astype(BF16)
    take_sides(0)
    for kk in (1, 2):
        @pl.when(me + 4 * kk < size)
        def _():
            for n in (0, 1):
                home_copy(n, kk).wait_recv()

        @pl.when(me + 4 * kk >= size)
        def _():
            for n in (0, 1):
                row[n, kk - 1] = jnp.zeros((DIM, TOK), BF16)
    for n, (to, scale) in enumerate(((dk, FACTOR), (dv, 1.0))):
        total = grads[n][0].astype(F32) + row[n, 0].astype(F32) + row[n, 1].astype(F32)
        to[...] = (total * scale).T

    for n in (0, 1):
        for at, copy in enumerate((column_copy(n, 1), column_copy(n, 2), relay_copy(n), far_copy(n, 9), far_copy(n, 10))):
            pl.when(down[at])(lambda: sent(copy))
        for kk in (0, 1, 2):
            sent(*row_copies(n, kk), onward_copy(n, kk), mid_copy(n, kk), side_copy(n, kk, 0), side_copy(n, kk, 1))
        for kk in (1, 2):
            pl.when(me >= 4 * kk)(lambda: sent(home_copy(n, kk)))
        for d in (9, 10):
            pl.when((me >= 12) & (x <= d - 9))(lambda: sent(tri_copy(n, d)))


def write_out(out_in, dq_in, dk_in, dv_in, out, dq, dk, dv):
    out[...] = out_in[...]
    dq[...] = dq_in[...].astype(F32)
    dk[...] = dk_in[...]
    dv[...] = dv_in[...]


def body(queries, keys, values, lengths, output_gradient):
    vmem = pl.BlockSpec(memory_space=pltpu.VMEM)
    wide = (TOK, HEADS * DIM)
    dma = pltpu.SemaphoreType.DMA
    out, dq, dk, dv = pl.pallas_call(
        kernel,
        out_shape=[
            jax.ShapeDtypeStruct(wide, BF16),
            jax.ShapeDtypeStruct(wide, BF16),
            jax.ShapeDtypeStruct((TOK, DIM), F32),
            jax.ShapeDtypeStruct((TOK, DIM), F32),
        ],
        in_specs=[vmem, vmem, vmem, pl.BlockSpec(memory_space=pltpu.SMEM), vmem],
        out_specs=[vmem] * 4,
        scratch_shapes=[
            pltpu.VMEM((SLOTS, TOK, DIM), BF16),
            pltpu.VMEM((SLOTS, TOK, DIM), BF16),
            pltpu.VMEM((HEADS, BLOCKS, TOK, TOK), F32),
            pltpu.VMEM((HEADS, BLOCKS, TOK, TOK), F32),
            pltpu.VMEM((HEADS, TOK, DIM), F32),
            pltpu.VMEM((HEADS, TOK, DIM), F32),
            pltpu.VMEM((HEADS, TOK, DIM), F32),
            pltpu.VMEM((HEADS, DIM, TOK), BF16),
            pltpu.VMEM((HEADS, DIM, TOK), BF16),
            pltpu.VMEM((TOK, DIM), jnp.int32),
            pltpu.VMEM((TOK, TOK), F32),
            pltpu.VMEM((SLOTS, DIM, TOK), BF16),
            pltpu.VMEM((SLOTS, DIM, TOK), BF16),
            pltpu.VMEM((2, 3, DIM, TOK), BF16),
            pltpu.VMEM((2, 3, 2, DIM, TOK), BF16),
            pltpu.VMEM((2, 2, DIM, TOK), BF16),
            pltpu.VMEM((2, 2, DIM, TOK), BF16),
            dma((2, 3, 3)),
            dma((2, SLOTS)),
            dma((2, 5)),
            dma((2, 3, 3)),
            dma((2, 3)),
            dma((2, 3, 2)),
            dma((2, 2)),
            dma((2, 4)),
            dma((2, 2)),
        ],
        compiler_params=pltpu.CompilerParams(
            collective_id=0, has_side_effects=True, vmem_limit_bytes=62 << 20
        ),
    )(queries, keys, values, lengths, output_gradient)
    return pl.pallas_call(
        write_out,
        out_shape=[
            jax.ShapeDtypeStruct(wide, BF16),
            jax.ShapeDtypeStruct(wide, F32),
            jax.ShapeDtypeStruct((TOK, DIM), F32),
            jax.ShapeDtypeStruct((TOK, DIM), F32),
        ],
        in_specs=[vmem] * 4,
        out_specs=[vmem] * 4,
    )(out, dq, dk, dv)


def solution(mesh):
    spec = P("ctx", "head")
    return jax.shard_map(
        body,
        mesh=mesh,
        in_specs=(spec, spec, spec, P(), spec),
        out_specs=(spec, spec, spec, spec),
        check_vma=False,
    )
```

```python
import jax
import jax.numpy as jnp
from jax import lax
from jax.experimental import pallas as pl
from jax.experimental.pallas import tpu as pltpu
from jax.sharding import PartitionSpec as P

HEADS = 8
TOK = 256
DIM = 128
BLOCKS = 11
SLOTS = 15
FACTOR = DIM ** -0.5
EXP2 = FACTOR * 1.4426950408889634
NEG = -1e30
MESH = pl.DeviceIdType.MESH
F32, BF16 = jnp.float32, jnp.bfloat16


def dot_nt(a, b):
    return lax.dot_general(a, b, (((1,), (1,)), ((), ())), preferred_element_type=F32)


def dot_nn(a, b):
    return lax.dot_general(a, b, (((1,), (0,)), ((), ())), preferred_element_type=F32)


def pick(table, column, step):
    value = jnp.int32(0)
    for at, entry in enumerate(table):
        if entry[column]:
            value = value + entry[column] * (step == at).astype(jnp.int32)
    return value


def kernel(q, k, v, lengths, g, out, dq, dk, dv,
           kb, vb, s_sc, d_sc, m_sc, dl_sc, acc_q, qt, gt, th, bias,
           gk, gv, mid, side, row, tri,
           f_send, f_recv, c_send, o_send, mid_recv, side_recv, row_recv, h_send, tri_recv):
    me = lax.axis_index("ctx")
    size = lax.axis_size("ctx")
    x = me % 4
    y = (me // 4) % 4
    base = me - x
    right, left = base + (x + 1) % 4, base + (x + 3) % 4
    stores = (kb, vb)

    def slot(kk, j, col):
        return (4 * kk + j - 4 * ((col + j) // 4) + SLOTS) % SLOTS

    def mine(kk, j):
        return slot(kk, j, (x + 4 - j) % 4)

    def remote(src, dst, send, recv, ctx):
        return pltpu.make_async_remote_copy(src_ref=src, dst_ref=dst, send_sem=send, recv_sem=recv,
                                            device_id={"ctx": ctx}, device_id_type=MESH)

    def start(*copies):
        for copy in copies:
            copy.start()

    def sent(*copies):
        for copy in copies:
            copy.wait_send()

    barrier = pltpu.get_barrier_semaphore()

    def greet(ctx):
        pl.semaphore_signal(barrier, inc=1, device_id={"ctx": ctx}, device_id_type=MESH)

    greet(right)
    greet(left)
    peers = 2
    for rows in (1, 2, 3):
        for sign in (1, -1):
            ctx = me + sign * 4 * rows
            on = (ctx >= 0) & (ctx < size)
            if rows == 3:
                on = on & (x <= 1)
            pl.when(on)(lambda ctx=ctx: greet(ctx))
            peers = peers + on.astype(jnp.int32)
    pl.semaphore_wait(barrier, peers)

    def column_copy(n, kk):
        src = (k, v)[n]
        return remote(src, stores[n].at[4 * kk], c_send.at[n, kk - 1], f_recv.at[n, 4 * kk], me + 4 * kk)

    def relay_copy(n):
        return remote(stores[n].at[4], stores[n].at[8], c_send.at[n, 2], f_recv.at[n, 8], me + 4)

    def far_copy(n, d):
        return remote(stores[n].at[d + 3], stores[n].at[d], c_send.at[n, d - 6], f_recv.at[n, d], me + 12)

    def row_copies(n, kk):
        buf = stores[n]
        copies = []
        for side_no, (j, ctx) in enumerate(((1, right), (3, left))):
            to = slot(kk, j, x)
            copies.append(remote(buf.at[4 * kk], buf.at[to], f_send.at[n, kk, side_no], f_recv.at[n, to], ctx))
        return copies

    def onward_copy(n, kk):
        buf, j, ctx = ((kb, 1, right), (vb, 3, left))[n]
        col = (x + 4 - j) % 4
        to = slot(kk, 2, col)
        return remote(buf.at[slot(kk, j, col)], buf.at[to], f_send.at[n, kk, 2], f_recv.at[n, to], ctx)

    def arrived(n, at):
        buf = stores[n]
        remote(buf.at[at], buf.at[at], f_send.at[n, 0, 0], f_recv.at[n, at], right).wait_recv()

    down = [(me + 4 < size), (me + 8 < size) & (y != 3), y == 0,
            (x == 0) & (me + 12 < size), (x <= 1) & (me + 12 < size)]

    @pl.when(down[0])
    def _():
        start(column_copy(0, 1), column_copy(1, 1))

    @pl.when(down[1])
    def _():
        start(column_copy(0, 2), column_copy(1, 2))

    kb[0] = k[...]
    vb[0] = v[...]
    start(*row_copies(0, 0), *row_copies(1, 0))

    for on, d in ((me < 4, 4), (me < 4, 8), ((me < 12) & (x == 0), 9), ((me < 12) & (x <= 1), 10)):
        @pl.when(on)
        def _():
            kb[d] = jnp.zeros((TOK, DIM), BF16)
            vb[d] = jnp.zeros((TOK, DIM), BF16)

    first = jnp.full((TOK, DIM), -1, jnp.int32) * (me * TOK)
    token = lax.broadcasted_iota(jnp.int32, (TOK, DIM), 0)
    end = -me * TOK
    for doc in range(lengths.shape[0]):
        end = end + lengths[doc]
        first = jnp.where(token >= end, end, first)
    th[...] = first
    for h in range(HEADS):
        cols = slice(h * DIM, (h + 1) * DIM)
        qt[h] = q[:, cols].T
        gt[h] = g[:, cols].T
    m_sc[...] = jnp.full_like(m_sc, NEG)

    def scores(d):
        key_at = lax.broadcasted_iota(jnp.int32, (TOK, DIM), 1) - d * TOK
        query_at = lax.broadcasted_iota(jnp.int32, (TOK, DIM), 0)
        for part in (0, 1):
            at = key_at + part * DIM
            seen = (at >= th[...]) & (at <= query_at)
            bias[:, part * DIM:(part + 1) * DIM] = jnp.where(seen, 0.0, NEG)
        key, value = kb[d], vb[d]
        for h in range(HEADS):
            cols = slice(h * DIM, (h + 1) * DIM)
            s = dot_nt(q[:, cols], key) + bias[...]
            s_sc[h, d] = s
            m_sc[h] = jnp.maximum(m_sc[h], jnp.maximum(s[:, :DIM], s[:, DIM:]))
            d_sc[h, d] = dot_nt(g[:, cols], value)

    def valid(kk, j):
        wraps = (j > x).astype(jnp.int32)
        d = 4 * kk + j - 4 * wraps
        return (d >= 0) & (d < BLOCKS), d

    def score_all(table):
        def step_of(step, _):
            ok, d = valid(pick(table, 0, step), pick(table, 1, step))

            @pl.when(ok)
            def _():
                scores(d)

            return 0

        lax.fori_loop(0, len(table), step_of, 0)

    score_all(((0, 0),))
    for n, j in ((0, 1), (1, 3)):
        arrived(n, mine(0, j))
        start(onward_copy(n, 0))
    for n in (0, 1):
        pl.when(me >= 4)(lambda: arrived(n, 4))
        start(*row_copies(n, 1))
        pl.when(down[2])(lambda: start(relay_copy(n)))
    arrived(1, mine(0, 1))
    arrived(0, mine(0, 3))
    pl.when(down[3])(lambda: start(far_copy(0, 9), far_copy(1, 9)))
    score_all(((1, 0), (0, 1)))
    for n in (0, 1):
        pl.when(me >= 4)(lambda: arrived(n, 8))
        start(*row_copies(n, 2))
    arrived(0, mine(0, 2))
    arrived(1, mine(0, 2))
    pl.when(down[4])(lambda: start(far_copy(0, 10), far_copy(1, 10)))
    score_all(((0, 3), (0, 2)))
    for n, j in ((0, 1), (1, 3)):
        arrived(n, mine(1, j))
        start(onward_copy(n, 1))
    arrived(1, mine(1, 1))
    arrived(0, mine(1, 3))
    score_all(((2, 0), (1, 1), (1, 3)))
    for n, j in ((0, 1), (1, 3)):
        arrived(n, mine(2, j))
        start(onward_copy(n, 2))
    arrived(1, mine(2, 1))
    arrived(0, mine(2, 3))
    arrived(0, mine(1, 2))
    arrived(1, mine(1, 2))
    score_all(((1, 2), (2, 1), (2, 3)))
    for d in (9, 10):
        @pl.when((me >= 12) & (x <= d - 9))
        def _():
            arrived(0, d)
            arrived(1, d)
    arrived(0, mine(2, 2))
    arrived(1, mine(2, 2))
    score_all(((3, 1), (3, 2), (2, 2)))

    def finish_head(h, _):
        m = jnp.max(m_sc[h], axis=1, keepdims=True)
        total = jnp.zeros((TOK, 2 * DIM), F32)
        ones = jnp.ones((TOK, DIM), BF16)
        for d in range(BLOCKS):
            p = jnp.exp2((s_sc[h, d] - m) * EXP2).astype(BF16)
            total = total + dot_nn(p, jnp.concatenate([vb[d], ones], 1))
        norm = total[:, DIM:]
        full = total[:, :DIM] / norm
        acc_q[h] = full
        m_sc[h] = m * EXP2 + jnp.log2(norm)
        return 0

    def finish_pair(i, _):
        finish_head(2 * i, 0)
        finish_head(2 * i + 1, 0)
        return 0

    lax.fori_loop(0, HEADS // 2, finish_pair, 0)
    for h in range(HEADS):
        cols = slice(h * DIM, (h + 1) * DIM)
        full = acc_q[h]
        out[:, cols] = full.astype(BF16)
        delta = jnp.sum(full * g[:, cols].astype(F32), axis=1, keepdims=True)
        dl_sc[h] = jnp.broadcast_to(delta, (TOK, DIM))
    acc_q[...] = jnp.zeros_like(acc_q)

    def gradients(d):
        key = kb[d]
        key_part = value_part = None
        for h in range(HEADS):
            lse, delta = m_sc[h], dl_sc[h]
            p = jnp.exp2(s_sc[h, d] * EXP2 - jnp.concatenate([lse, lse], 1))
            ds = (p * (d_sc[h, d] - jnp.concatenate([delta, delta], 1))).astype(BF16)
            acc_q[h] += dot_nn(ds, key)
            a, b = dot_nn(qt[h], ds), dot_nn(gt[h], p.astype(BF16))
            key_part = a if h == 0 else key_part + a
            value_part = b if h == 0 else value_part + b
        gk[d] = key_part.astype(BF16)
        gv[d] = value_part.astype(BF16)

    grads = (gk, gv)

    def add(ref, at, *others):
        total = ref[at].astype(F32)
        for other in others:
            total = total + other.astype(F32)
        ref[at] = total.astype(BF16)

    def mid_copy(n, kk):
        return remote(grads[n].at[mine(kk, 2)], mid.at[n, kk], o_send.at[n, kk, 2], mid_recv.at[n, kk], (left, right)[n])

    def side_copy(n, kk, side_no):
        at, ctx = mine(kk, (1, 3)[side_no]), (left, right)[side_no]
        return remote(grads[n].at[at], side.at[n, kk, side_no], o_send.at[n, kk, side_no],
                      side_recv.at[n, kk, side_no], ctx)

    def home_copy(n, kk):
        return remote(grads[n].at[4 * kk], row.at[n, kk - 1], h_send.at[n, kk - 1], row_recv.at[n, kk - 1], me - 4 * kk)

    def tri_copy(n, d):
        return remote(grads[n].at[d], tri.at[n, d - 9], h_send.at[n, d - 7], tri_recv.at[n, d - 9], me - 12)

    def gradients_all(table):
        def step_of(step, _):
            kk, j = pick(table, 0, step), pick(table, 1, step)
            ok, d = valid(kk, j)
            there = (d + SLOTS) % SLOTS

            @pl.when(ok)
            def _():
                gradients(d)

            @pl.when(jnp.logical_not(ok) & (kk < 3))
            def _():
                gk[there] = jnp.zeros((DIM, TOK), BF16)
                gv[there] = jnp.zeros((DIM, TOK), BF16)

            return 0

        lax.fori_loop(0, len(table), step_of, 0)

    def pass_sides(kk):
        start(side_copy(1, kk, 0), side_copy(0, kk, 1))
        for n, j in ((0, 1), (1, 3)):
            mid_copy(n, kk).wait_recv()
            add(grads[n], mine(kk, j), mid[n, kk])
            start(side_copy(n, kk, n))

    def take_sides(kk):
        for n in (0, 1):
            side_copy(n, kk, 0).wait_recv()
            side_copy(n, kk, 1).wait_recv()
            add(grads[n], 4 * kk, side[n, kk, 0], side[n, kk, 1])
            if kk:
                pl.when(me >= 4 * kk)(lambda: start(home_copy(n, kk)))

    for d, block in ((10, (3, 2)), (9, (3, 1))):
        gradients_all((block,))
        pl.when((me >= 12) & (x <= d - 9))(lambda: start(tri_copy(0, d), tri_copy(1, d)))
    gradients_all(((2, 2),))
    start(mid_copy(0, 2), mid_copy(1, 2))
    gradients_all(((1, 2),))
    start(mid_copy(0, 1), mid_copy(1, 1))
    gradients_all(((2, 1), (2, 3)))
    pass_sides(2)
    gradients_all(((1, 1), (1, 3)))
    pass_sides(1)
    gradients_all(((0, 2), (2, 0), (1, 0), (0, 1), (0, 3), (0, 0)))
    take_sides(2)

    @pl.when((me + 12 < size) & (x <= 1))
    def _():
        for n in (0, 1):
            tri_copy(n, 10).wait_recv()
            grads[n][13] = tri[n, 1]

    start(mid_copy(0, 0), mid_copy(1, 0))
    take_sides(1)

    @pl.when((me + 12 < size) & (x <= 0))
    def _():
        for n in (0, 1):
            tri_copy(n, 9).wait_recv()
            grads[n][12] = tri[n, 0]

    pass_sides(0)

    for h in range(HEADS):
        dq[:, h * DIM:(h + 1) * DIM] = (acc_q[h] * FACTOR).astype(BF16)
    take_sides(0)
    for kk in (1, 2):
        @pl.when(me + 4 * kk < size)
        def _():
            for n in (0, 1):
                home_copy(n, kk).wait_recv()

        @pl.when(me + 4 * kk >= size)
        def _():
            for n in (0, 1):
                row[n, kk - 1] = jnp.zeros((DIM, TOK), BF16)
    for n, (to, scale) in enumerate(((dk, FACTOR), (dv, 1.0))):
        total = grads[n][0].astype(F32) + row[n, 0].astype(F32) + row[n, 1].astype(F32)
        to[...] = (total * scale).T

    for n in (0, 1):
        for at, copy in enumerate((column_copy(n, 1), column_copy(n, 2), relay_copy(n), far_copy(n, 9), far_copy(n, 10))):
            pl.when(down[at])(lambda: sent(copy))
        for kk in (0, 1, 2):
            sent(*row_copies(n, kk), onward_copy(n, kk), mid_copy(n, kk), side_copy(n, kk, 0), side_copy(n, kk, 1))
        for kk in (1, 2):
            pl.when(me >= 4 * kk)(lambda: sent(home_copy(n, kk)))
        for d in (9, 10):
            pl.when((me >= 12) & (x <= d - 9))(lambda: sent(tri_copy(n, d)))


def write_out(out_in, dq_in, dk_in, dv_in, out, dq, dk, dv):
    out[...] = out_in[...]
    dq[...] = dq_in[...].astype(F32)
    dk[...] = dk_in[...]
    dv[...] = dv_in[...]


def body(queries, keys, values, lengths, output_gradient):
    vmem = pl.BlockSpec(memory_space=pltpu.VMEM)
    wide = (TOK, HEADS * DIM)
    dma = pltpu.SemaphoreType.DMA
    out, dq, dk, dv = pl.pallas_call(
        kernel,
        out_shape=[
            jax.ShapeDtypeStruct(wide, BF16),
            jax.ShapeDtypeStruct(wide, BF16),
            jax.ShapeDtypeStruct((TOK, DIM), F32),
            jax.ShapeDtypeStruct((TOK, DIM), F32),
        ],
        in_specs=[vmem, vmem, vmem, pl.BlockSpec(memory_space=pltpu.SMEM), vmem],
        out_specs=[vmem] * 4,
        scratch_shapes=[
            pltpu.VMEM((SLOTS, TOK, DIM), BF16),
            pltpu.VMEM((SLOTS, TOK, DIM), BF16),
            pltpu.VMEM((HEADS, BLOCKS, TOK, TOK), F32),
            pltpu.VMEM((HEADS, BLOCKS, TOK, TOK), F32),
            pltpu.VMEM((HEADS, TOK, DIM), F32),
            pltpu.VMEM((HEADS, TOK, DIM), F32),
            pltpu.VMEM((HEADS, TOK, DIM), F32),
            pltpu.VMEM((HEADS, DIM, TOK), BF16),
            pltpu.VMEM((HEADS, DIM, TOK), BF16),
            pltpu.VMEM((TOK, DIM), jnp.int32),
            pltpu.VMEM((TOK, TOK), F32),
            pltpu.VMEM((SLOTS, DIM, TOK), BF16),
            pltpu.VMEM((SLOTS, DIM, TOK), BF16),
            pltpu.VMEM((2, 3, DIM, TOK), BF16),
            pltpu.VMEM((2, 3, 2, DIM, TOK), BF16),
            pltpu.VMEM((2, 2, DIM, TOK), BF16),
            pltpu.VMEM((2, 2, DIM, TOK), BF16),
            dma((2, 3, 3)),
            dma((2, SLOTS)),
            dma((2, 5)),
            dma((2, 3, 3)),
            dma((2, 3)),
            dma((2, 3, 2)),
            dma((2, 2)),
            dma((2, 4)),
            dma((2, 2)),
        ],
        compiler_params=pltpu.CompilerParams(
            collective_id=0, has_side_effects=True, vmem_limit_bytes=62 << 20
        ),
    )(queries, keys, values, lengths, output_gradient)
    return pl.pallas_call(
        write_out,
        out_shape=[
            jax.ShapeDtypeStruct(wide, BF16),
            jax.ShapeDtypeStruct(wide, F32),
            jax.ShapeDtypeStruct((TOK, DIM), F32),
            jax.ShapeDtypeStruct((TOK, DIM), F32),
        ],
        in_specs=[vmem] * 4,
        out_specs=[vmem] * 4,
    )(out, dq, dk, dv)


def solution(mesh):
    spec = P("ctx", "head")
    return jax.shard_map(
        body,
        mesh=mesh,
        in_specs=(spec, spec, spec, P(), spec),
        out_specs=(spec, spec, spec, spec),
        check_vma=False,
    )
```

```python
import jax
import jax.numpy as jnp
from jax import lax
from jax.experimental import pallas as pl
from jax.experimental.pallas import tpu as pltpu
from jax.sharding import PartitionSpec as P

HEADS = 8
TOK = 256
DIM = 128
BLOCKS = 11
SLOTS = 15
FACTOR = DIM ** -0.5
EXP2 = FACTOR * 1.4426950408889634
NEG = -1e30
MESH = pl.DeviceIdType.MESH
F32, BF16 = jnp.float32, jnp.bfloat16


def dot_nt(a, b):
    return lax.dot_general(a, b, (((1,), (1,)), ((), ())), preferred_element_type=F32)


def dot_nn(a, b):
    return lax.dot_general(a, b, (((1,), (0,)), ((), ())), preferred_element_type=F32)


def pick(table, column, step):
    value = jnp.int32(0)
    for at, entry in enumerate(table):
        if entry[column]:
            value = value + entry[column] * (step == at).astype(jnp.int32)
    return value


def kernel(q_in, k, v, lengths, g_in, out, dq, dk, dv,
           q, g, load_sem,
           kb, vb, s_sc, d_sc, m_sc, dl_sc, acc_q, qt, gt, th, bias,
           gk, gv, mid, side, row, tri,
           f_send, f_recv, c_send, o_send, mid_recv, side_recv, row_recv, h_send, tri_recv):
    me = lax.axis_index("ctx")
    size = lax.axis_size("ctx")
    x = me % 4
    y = (me // 4) % 4
    base = me - x
    right, left = base + (x + 1) % 4, base + (x + 3) % 4
    stores = (kb, vb)

    def slot(kk, j, col):
        return (4 * kk + j - 4 * ((col + j) // 4) + SLOTS) % SLOTS

    def mine(kk, j):
        return slot(kk, j, (x + 4 - j) % 4)

    def remote(src, dst, send, recv, ctx):
        return pltpu.make_async_remote_copy(src_ref=src, dst_ref=dst, send_sem=send, recv_sem=recv,
                                            device_id={"ctx": ctx}, device_id_type=MESH)

    def start(*copies):
        for copy in copies:
            copy.start()

    def sent(*copies):
        for copy in copies:
            copy.wait_send()

    loads = [pltpu.make_async_copy(q_in, q, load_sem.at[0]), pltpu.make_async_copy(g_in, g, load_sem.at[1])]
    barrier = pltpu.get_barrier_semaphore()

    def greet(ctx):
        pl.semaphore_signal(barrier, inc=1, device_id={"ctx": ctx}, device_id_type=MESH)

    greet(right)
    greet(left)
    peers = 2
    for rows in (1, 2, 3):
        for sign in (1, -1):
            ctx = me + sign * 4 * rows
            on = (ctx >= 0) & (ctx < size)
            if rows == 3:
                on = on & (x <= 1)
            pl.when(on)(lambda ctx=ctx: greet(ctx))
            peers = peers + on.astype(jnp.int32)
    start(*loads)
    pl.semaphore_wait(barrier, peers)

    def column_copy(n, kk):
        src = (k, v)[n]
        return remote(src, stores[n].at[4 * kk], c_send.at[n, kk - 1], f_recv.at[n, 4 * kk], me + 4 * kk)

    def relay_copy(n):
        return remote(stores[n].at[4], stores[n].at[8], c_send.at[n, 2], f_recv.at[n, 8], me + 4)

    def far_copy(n, d):
        return remote(stores[n].at[d + 3], stores[n].at[d], c_send.at[n, d - 6], f_recv.at[n, d], me + 12)

    def row_copies(n, kk):
        buf = stores[n]
        copies = []
        for side_no, (j, ctx) in enumerate(((1, right), (3, left))):
            to = slot(kk, j, x)
            copies.append(remote(buf.at[4 * kk], buf.at[to], f_send.at[n, kk, side_no], f_recv.at[n, to], ctx))
        return copies

    def onward_copy(n, kk):
        buf, j, ctx = ((kb, 1, right), (vb, 3, left))[n]
        col = (x + 4 - j) % 4
        to = slot(kk, 2, col)
        return remote(buf.at[slot(kk, j, col)], buf.at[to], f_send.at[n, kk, 2], f_recv.at[n, to], ctx)

    def arrived(n, at):
        buf = stores[n]
        remote(buf.at[at], buf.at[at], f_send.at[n, 0, 0], f_recv.at[n, at], right).wait_recv()

    down = [(me + 4 < size), (me + 8 < size) & (y != 3), y == 0,
            (x == 0) & (me + 12 < size), (x <= 1) & (me + 12 < size)]

    @pl.when(down[0])
    def _():
        start(column_copy(0, 1), column_copy(1, 1))

    @pl.when(down[1])
    def _():
        start(column_copy(0, 2), column_copy(1, 2))

    kb[0] = k[...]
    vb[0] = v[...]
    start(*row_copies(0, 0), *row_copies(1, 0))

    for on, d in ((me < 4, 4), (me < 4, 8), ((me < 12) & (x == 0), 9), ((me < 12) & (x <= 1), 10)):
        @pl.when(on)
        def _():
            kb[d] = jnp.zeros((TOK, DIM), BF16)
            vb[d] = jnp.zeros((TOK, DIM), BF16)

    for load in loads:
        load.wait()

    first = jnp.full((TOK, DIM), -1, jnp.int32) * (me * TOK)
    token = lax.broadcasted_iota(jnp.int32, (TOK, DIM), 0)
    end = -me * TOK
    for doc in range(lengths.shape[0]):
        end = end + lengths[doc]
        first = jnp.where(token >= end, end, first)
    th[...] = first
    for h in range(HEADS):
        cols = slice(h * DIM, (h + 1) * DIM)
        qt[h] = q[:, cols].T
        gt[h] = g[:, cols].T
    m_sc[...] = jnp.full_like(m_sc, NEG)

    def scores(d):
        key_at = lax.broadcasted_iota(jnp.int32, (TOK, DIM), 1) - d * TOK
        query_at = lax.broadcasted_iota(jnp.int32, (TOK, DIM), 0)
        for part in (0, 1):
            at = key_at + part * DIM
            seen = (at >= th[...]) & (at <= query_at)
            bias[:, part * DIM:(part + 1) * DIM] = jnp.where(seen, 0.0, NEG)
        key, value = kb[d], vb[d]
        for h in range(HEADS):
            cols = slice(h * DIM, (h + 1) * DIM)
            s = dot_nt(q[:, cols], key) + bias[...]
            s_sc[h, d] = s
            m_sc[h] = jnp.maximum(m_sc[h], jnp.maximum(s[:, :DIM], s[:, DIM:]))
            d_sc[h, d] = dot_nt(g[:, cols], value)

    def valid(kk, j):
        wraps = (j > x).astype(jnp.int32)
        d = 4 * kk + j - 4 * wraps
        return (d >= 0) & (d < BLOCKS), d

    def score_all(table):
        def step_of(step, _):
            ok, d = valid(pick(table, 0, step), pick(table, 1, step))

            @pl.when(ok)
            def _():
                scores(d)

            return 0

        lax.fori_loop(0, len(table), step_of, 0)

    score_all(((0, 0),))
    for n, j in ((0, 1), (1, 3)):
        arrived(n, mine(0, j))
        start(onward_copy(n, 0))
    for n in (0, 1):
        pl.when(me >= 4)(lambda: arrived(n, 4))
        start(*row_copies(n, 1))
        pl.when(down[2])(lambda: start(relay_copy(n)))
    arrived(1, mine(0, 1))
    arrived(0, mine(0, 3))
    pl.when(down[3])(lambda: start(far_copy(0, 9), far_copy(1, 9)))
    score_all(((1, 0), (0, 1)))
    for n in (0, 1):
        pl.when(me >= 4)(lambda: arrived(n, 8))
        start(*row_copies(n, 2))
    arrived(0, mine(0, 2))
    arrived(1, mine(0, 2))
    pl.when(down[4])(lambda: start(far_copy(0, 10), far_copy(1, 10)))
    score_all(((0, 3), (0, 2)))
    for n, j in ((0, 1), (1, 3)):
        arrived(n, mine(1, j))
        start(onward_copy(n, 1))
    arrived(1, mine(1, 1))
    arrived(0, mine(1, 3))
    score_all(((2, 0), (1, 1), (1, 3)))
    for n, j in ((0, 1), (1, 3)):
        arrived(n, mine(2, j))
        start(onward_copy(n, 2))
    arrived(1, mine(2, 1))
    arrived(0, mine(2, 3))
    arrived(0, mine(1, 2))
    arrived(1, mine(1, 2))
    score_all(((1, 2), (2, 1), (2, 3)))
    for d in (9, 10):
        @pl.when((me >= 12) & (x <= d - 9))
        def _():
            arrived(0, d)
            arrived(1, d)
    arrived(0, mine(2, 2))
    arrived(1, mine(2, 2))
    score_all(((3, 1), (3, 2), (2, 2)))

    def finish_head(h, _):
        m = jnp.max(m_sc[h], axis=1, keepdims=True)
        total = jnp.zeros((TOK, 2 * DIM), F32)
        ones = jnp.ones((TOK, DIM), BF16)
        for d in range(BLOCKS):
            p = jnp.exp2((s_sc[h, d] - m) * EXP2).astype(BF16)
            total = total + dot_nn(p, jnp.concatenate([vb[d], ones], 1))
        norm = total[:, DIM:]
        full = total[:, :DIM] / norm
        acc_q[h] = full
        m_sc[h] = m * EXP2 + jnp.log2(norm)
        return 0

    def finish_pair(i, _):
        finish_head(2 * i, 0)
        finish_head(2 * i + 1, 0)
        return 0

    lax.fori_loop(0, HEADS // 2, finish_pair, 0)
    for h in range(HEADS):
        cols = slice(h * DIM, (h + 1) * DIM)
        full = acc_q[h]
        out[:, cols] = full.astype(BF16)
        delta = jnp.sum(full * g[:, cols].astype(F32), axis=1, keepdims=True)
        dl_sc[h] = jnp.broadcast_to(delta, (TOK, DIM))
    acc_q[...] = jnp.zeros_like(acc_q)

    def gradients(d):
        key = kb[d]
        key_part = value_part = None
        for h in range(HEADS):
            lse, delta = m_sc[h], dl_sc[h]
            p = jnp.exp2(s_sc[h, d] * EXP2 - jnp.concatenate([lse, lse], 1))
            ds = (p * (d_sc[h, d] - jnp.concatenate([delta, delta], 1))).astype(BF16)
            acc_q[h] += dot_nn(ds, key)
            a, b = dot_nn(qt[h], ds), dot_nn(gt[h], p.astype(BF16))
            key_part = a if h == 0 else key_part + a
            value_part = b if h == 0 else value_part + b
        gk[d] = key_part.astype(BF16)
        gv[d] = value_part.astype(BF16)

    grads = (gk, gv)

    def add(ref, at, *others):
        total = ref[at].astype(F32)
        for other in others:
            total = total + other.astype(F32)
        ref[at] = total.astype(BF16)

    def mid_copy(n, kk):
        return remote(grads[n].at[mine(kk, 2)], mid.at[n, kk], o_send.at[n, kk, 2], mid_recv.at[n, kk], (left, right)[n])

    def side_copy(n, kk, side_no):
        at, ctx = mine(kk, (1, 3)[side_no]), (left, right)[side_no]
        return remote(grads[n].at[at], side.at[n, kk, side_no], o_send.at[n, kk, side_no],
                      side_recv.at[n, kk, side_no], ctx)

    def home_copy(n, kk):
        return remote(grads[n].at[4 * kk], row.at[n, kk - 1], h_send.at[n, kk - 1], row_recv.at[n, kk - 1], me - 4 * kk)

    def tri_copy(n, d):
        return remote(grads[n].at[d], tri.at[n, d - 9], h_send.at[n, d - 7], tri_recv.at[n, d - 9], me - 12)

    def gradients_all(table):
        def step_of(step, _):
            kk, j = pick(table, 0, step), pick(table, 1, step)
            ok, d = valid(kk, j)
            there = (d + SLOTS) % SLOTS

            @pl.when(ok)
            def _():
                gradients(d)

            @pl.when(jnp.logical_not(ok) & (kk < 3))
            def _():
                gk[there] = jnp.zeros((DIM, TOK), BF16)
                gv[there] = jnp.zeros((DIM, TOK), BF16)

            return 0

        lax.fori_loop(0, len(table), step_of, 0)

    def pass_sides(kk):
        start(side_copy(1, kk, 0), side_copy(0, kk, 1))
        for n, j in ((0, 1), (1, 3)):
            mid_copy(n, kk).wait_recv()
            add(grads[n], mine(kk, j), mid[n, kk])
            start(side_copy(n, kk, n))

    def take_sides(kk):
        for n in (0, 1):
            side_copy(n, kk, 0).wait_recv()
            side_copy(n, kk, 1).wait_recv()
            add(grads[n], 4 * kk, side[n, kk, 0], side[n, kk, 1])
            if kk:
                pl.when(me >= 4 * kk)(lambda: start(home_copy(n, kk)))

    for d, block in ((10, (3, 2)), (9, (3, 1))):
        gradients_all((block,))
        pl.when((me >= 12) & (x <= d - 9))(lambda: start(tri_copy(0, d), tri_copy(1, d)))
    gradients_all(((2, 2),))
    start(mid_copy(0, 2), mid_copy(1, 2))
    gradients_all(((1, 2),))
    start(mid_copy(0, 1), mid_copy(1, 1))
    gradients_all(((2, 1), (2, 3)))
    pass_sides(2)
    gradients_all(((1, 1), (1, 3)))
    pass_sides(1)
    gradients_all(((0, 2), (2, 0), (1, 0), (0, 1), (0, 3), (0, 0)))
    take_sides(2)

    @pl.when((me + 12 < size) & (x <= 1))
    def _():
        for n in (0, 1):
            tri_copy(n, 10).wait_recv()
            grads[n][13] = tri[n, 1]

    start(mid_copy(0, 0), mid_copy(1, 0))
    take_sides(1)

    @pl.when((me + 12 < size) & (x <= 0))
    def _():
        for n in (0, 1):
            tri_copy(n, 9).wait_recv()
            grads[n][12] = tri[n, 0]

    pass_sides(0)

    for h in range(HEADS):
        dq[:, h * DIM:(h + 1) * DIM] = (acc_q[h] * FACTOR).astype(BF16)
    take_sides(0)
    for kk in (1, 2):
        @pl.when(me + 4 * kk < size)
        def _():
            for n in (0, 1):
                home_copy(n, kk).wait_recv()

        @pl.when(me + 4 * kk >= size)
        def _():
            for n in (0, 1):
                row[n, kk - 1] = jnp.zeros((DIM, TOK), BF16)
    for n, (to, scale) in enumerate(((dk, FACTOR), (dv, 1.0))):
        total = grads[n][0].astype(F32) + row[n, 0].astype(F32) + row[n, 1].astype(F32)
        to[...] = (total * scale).T

    for n in (0, 1):
        for at, copy in enumerate((column_copy(n, 1), column_copy(n, 2), relay_copy(n), far_copy(n, 9), far_copy(n, 10))):
            pl.when(down[at])(lambda: sent(copy))
        for kk in (0, 1, 2):
            sent(*row_copies(n, kk), onward_copy(n, kk), mid_copy(n, kk), side_copy(n, kk, 0), side_copy(n, kk, 1))
        for kk in (1, 2):
            pl.when(me >= 4 * kk)(lambda: sent(home_copy(n, kk)))
        for d in (9, 10):
            pl.when((me >= 12) & (x <= d - 9))(lambda: sent(tri_copy(n, d)))


def write_out(out_in, dq_in, dk_in, dv_in, out, dq, dk, dv):
    out[...] = out_in[...]
    dq[...] = dq_in[...].astype(F32)
    dk[...] = dk_in[...]
    dv[...] = dv_in[...]


def body(queries, keys, values, lengths, output_gradient):
    vmem = pl.BlockSpec(memory_space=pltpu.VMEM)
    whole = pl.BlockSpec(memory_space=pl.ANY)
    wide = (TOK, HEADS * DIM)
    dma = pltpu.SemaphoreType.DMA
    out, dq, dk, dv = pl.pallas_call(
        kernel,
        out_shape=[
            jax.ShapeDtypeStruct(wide, BF16),
            jax.ShapeDtypeStruct(wide, BF16),
            jax.ShapeDtypeStruct((TOK, DIM), F32),
            jax.ShapeDtypeStruct((TOK, DIM), F32),
        ],
        in_specs=[whole, vmem, vmem, pl.BlockSpec(memory_space=pltpu.SMEM), whole],
        out_specs=[vmem] * 4,
        scratch_shapes=[
            pltpu.VMEM(wide, BF16),
            pltpu.VMEM(wide, BF16),
            dma((2,)),
            pltpu.VMEM((SLOTS, TOK, DIM), BF16),
            pltpu.VMEM((SLOTS, TOK, DIM), BF16),
            pltpu.VMEM((HEADS, BLOCKS, TOK, TOK), F32),
            pltpu.VMEM((HEADS, BLOCKS, TOK, TOK), F32),
            pltpu.VMEM((HEADS, TOK, DIM), F32),
            pltpu.VMEM((HEADS, TOK, DIM), F32),
            pltpu.VMEM((HEADS, TOK, DIM), F32),
            pltpu.VMEM((HEADS, DIM, TOK), BF16),
            pltpu.VMEM((HEADS, DIM, TOK), BF16),
            pltpu.VMEM((TOK, DIM), jnp.int32),
            pltpu.VMEM((TOK, TOK), F32),
            pltpu.VMEM((SLOTS, DIM, TOK), BF16),
            pltpu.VMEM((SLOTS, DIM, TOK), BF16),
            pltpu.VMEM((2, 3, DIM, TOK), BF16),
            pltpu.VMEM((2, 3, 2, DIM, TOK), BF16),
            pltpu.VMEM((2, 2, DIM, TOK), BF16),
            pltpu.VMEM((2, 2, DIM, TOK), BF16),
            dma((2, 3, 3)),
            dma((2, SLOTS)),
            dma((2, 5)),
            dma((2, 3, 3)),
            dma((2, 3)),
            dma((2, 3, 2)),
            dma((2, 2)),
            dma((2, 4)),
            dma((2, 2)),
        ],
        compiler_params=pltpu.CompilerParams(
            collective_id=0, has_side_effects=True, vmem_limit_bytes=62 << 20
        ),
    )(queries, keys, values, lengths, output_gradient)
    return pl.pallas_call(
        write_out,
        out_shape=[
            jax.ShapeDtypeStruct(wide, BF16),
            jax.ShapeDtypeStruct(wide, F32),
            jax.ShapeDtypeStruct((TOK, DIM), F32),
            jax.ShapeDtypeStruct((TOK, DIM), F32),
        ],
        in_specs=[vmem] * 4,
        out_specs=[vmem] * 4,
    )(out, dq, dk, dv)


def solution(mesh):
    spec = P("ctx", "head")
    return jax.shard_map(
        body,
        mesh=mesh,
        in_specs=(spec, spec, spec, P(), spec),
        out_specs=(spec, spec, spec, spec),
        check_vma=False,
    )
```
